768 devices in a mesh: dp: 24 (over z, x_hi), seq: 32 (over x_lo, y, core).
Axes of the slice: x: 4 (x_hi: 2, x_lo: 2; x = x_hi * 2 + x_lo), y: 8, z: 12, core: 2. Of those that a mesh axis runs over, the one named last changes fastest.
Arguments:
- query_rows: bfloat16 [98304, 2048], P(('dp', 'seq')), may hold values from -30 to 30, as said below
- key_rows: bfloat16 [98304, 2048], P(('dp', 'seq')), may hold values from -4 to 4
- value_rows: bfloat16 [98304, 2048], P(('dp', 'seq')), may hold values from -6 to 6
- clip_tiles: int32 [24, 32], P('dp'), may hold values from 0 to 3, never falling along the last dimension, each value on 1 to 16 neighbouring positions
- conditioning: bfloat16 [96, 3072], P(None, 'dp'), may hold values from -8 to 8
- gate_weight: bfloat16 [3072, 2048], P('dp', 'seq'), may hold values from -0.109375 to 0.109375
Outputs:
- attention_out: bfloat16 [98304, 2048], P(('dp', 'seq'))
The draws below stay inside these ranges and needn't reach their ends.
Inputs may be any that keep to these rules, and one draw needn't show every extreme that they name: `query_rows`: entries of order one; a few rows are far larger. `clip_tiles`: clip numbers never fall along the tiles of a pack; every clip of 0 to 3 holds 1 to 16 tiles.
All inputs are finite; a program needn't handle non-finite values.
Results may differ from the reference program's by a relative error of at most 0.02.
Values may be sent and summed in bfloat16 or wider, within the bound.
A program may use at most 32 MiB of HBM per device.

```python
import math
import jax
import jax.numpy as jnp
import numpy as np
from jax import lax

D = 3072
HEADS = 16
HD = 128
TILE = 128
TOK = 128
TILES = 32
CLIPS = 4
MOST = 16
TOKENS = 98304
N_DP = 24
N_SEQ = 32


def draw_query_rows(key, part):
    key = jax.random.fold_in(key, 11)
    total_rows = N_DP * TOK * N_SEQ
    base = 1.5 * jax.random.truncated_normal(key, -4.0, 4.0, (total_rows, HEADS * HD), jnp.float32)
    return base.astype(jnp.bfloat16)


def draw_key_rows(key, part):
    key = jax.random.fold_in(key, 12)
    total_rows = N_DP * TOK * N_SEQ
    base = jax.random.truncated_normal(key, -4.0, 4.0, (total_rows, HEADS * HD), jnp.float32)
    return base.astype(jnp.bfloat16)


def shard_levels(stream_key, dims, pieces, smallest, high):
    gain = 1.0
    for axis_at, parts in pieces:
        draws = jax.random.uniform(jax.random.fold_in(jax.random.fold_in(stream_key, 6), axis_at), (parts,), jnp.float32, smallest / len(pieces), high / len(pieces))
        gain = gain * jnp.repeat(jnp.exp(draws), dims[axis_at] // parts).reshape((-1,) + (1,) * (len(dims) - 1 - axis_at))
    return gain


def split_up(number_of, total, limit, slope):
    loads = [(1 << 20) // math.isqrt(standing ** slope) + 1 for standing in range(2, number_of + 1)]
    rest, given = total - limit - (number_of - 1), [1] * (number_of - 1)
    while rest > 0:
        free = [i for i in range(number_of - 1) if given[i] < limit]
        whole, remaining = sum([loads[i] for i in free]), rest
        for i in free:
            addition = min(limit - given[i], max(1, remaining * loads[i] // whole), rest)
            given[i] = given[i] + addition
            rest = rest - addition
    return np.array([limit] + given)


def ragged_sizes(stream_key, number_of, total, reach, slope):
    if number_of == 2:
        one = jax.random.randint(stream_key, (), max(1, total - reach), min(reach, total - 1) + 1)
        return jnp.stack([one, total - one])
    tallies = jnp.asarray(split_up(number_of, total, reach, slope), jnp.int32)
    twos = (number_of - 1) // 2
    donor, taker = tallies[1:1 + 2 * twos:2], tallies[2:2 + 2 * twos:2]
    margin = jnp.minimum(donor - 1, reach - taker)
    moved = jax.random.randint(jax.random.fold_in(stream_key, 1), (twos,), 0, 1 << 20) % (margin + 1)
    tallies = tallies.at[1:1 + 2 * twos:2].set(donor - moved).at[2:2 + 2 * twos:2].set(taker + moved)
    return tallies[jax.random.permutation(jax.random.fold_in(stream_key, 2), number_of)]


def bell_draw(own_key, dims, scale, bound, cuts=(), dtype=jnp.bfloat16):
    loudness = shard_levels(own_key, dims, cuts, -0.22, 0.18) if cuts else 1.0
    entries = jax.random.normal(own_key, dims, jnp.float32) * scale * loudness
    return jnp.minimum(jnp.maximum(entries, -bound), bound).astype(dtype)


def setup_inputs(seed: int = 0) -> dict:
    splits = jax.random.split(jax.random.key(seed), 7)
    query_rows = draw_query_rows(jax.random.fold_in(splits[6], 71), 0)
    key_rows = draw_key_rows(jax.random.fold_in(splits[6], 71), 0)
    value_rows = bell_draw(splits[2], (TOKENS, HEADS * HD), 1.0, 6.0, ((0, 768),))
    clip_tiles = jax.vmap(lambda own: jnp.searchsorted(jnp.cumsum(ragged_sizes(own, CLIPS, TILES, MOST, 0)), jnp.arange(TILES), side="right"))(jax.random.split(splits[3], N_DP)).reshape((N_DP, TILES)).astype(jnp.int32)
    conditioning = bell_draw(splits[4], (N_DP * CLIPS, D), 2.0, 8.0, ((1, 24),))
    gate_weight = bell_draw(splits[5], (D, HEADS * HD), D ** -0.5, 0.109375, ((0, 24), (1, 32)))
    return {"query_rows": query_rows, "key_rows": key_rows, "value_rows": value_rows, "clip_tiles": clip_tiles, "conditioning": conditioning, "gate_weight": gate_weight}


def reference(query_rows, key_rows, value_rows, clip_tiles, conditioning, gate_weight):
    packs = clip_tiles.shape[0]
    width = query_rows.shape[1]
    heads = width // HD
    scale = 1.0 / math.sqrt(HD)
    act = jax.nn.silu(conditioning.astype(jnp.float32)).astype(jnp.bfloat16)
    gates = jnp.dot(act, gate_weight, preferred_element_type=jnp.float32).reshape(packs, -1, width)

    def split_heads(array):
        return array.reshape(packs, -1, heads, HD).transpose(0, 2, 1, 3)

    def one_pack(inputs):
        query_pack, key_pack, value_pack, tiles, gate_pack = inputs
        token_clip = jnp.repeat(tiles, TILE)
        same = token_clip[:, None] == token_clip[None, :]

        def one_head(head_in):
            query_head, key_head, value_head = head_in
            scores = jnp.dot(query_head, key_head.T, preferred_element_type=jnp.float32) * scale
            masked = jnp.where(same, scores, -1e+30)
            top = masked.max(axis=1, keepdims=True)
            weights = jnp.where(same, jnp.exp(masked - top), 0.0)
            total = weights.sum(axis=1, keepdims=True)
            summed = jnp.dot(weights.astype(jnp.bfloat16), value_head, preferred_element_type=jnp.float32)
            return summed / total
        attended = lax.map(one_head, (query_pack, key_pack, value_pack))
        attended = attended.transpose(1, 0, 2).reshape(-1, width)
        gate_rows = jnp.take(gate_pack, token_clip, axis=0)
        return (attended * gate_rows).astype(jnp.bfloat16)
    result = lax.map(one_pack, (split_heads(query_rows), split_heads(key_rows), split_heads(value_rows), clip_tiles, gates))
    return result.reshape(-1, width)
```

```python
import functools
import math

import jax
import jax.numpy as jnp
from jax import lax
from jax.experimental import pallas as pl
from jax.experimental.pallas import tpu as pltpu
from jax.sharding import PartitionSpec as P

HD = 128
TILE = 128
CLIPS = 4
CHUNK = 2
LOG2E = 1.4426950408889634
MESH = pl.DeviceIdType.MESH


def remote(src, dst, send_sem, recv_sem, device):
    return pltpu.make_async_remote_copy(
        src_ref=src,
        dst_ref=dst,
        send_sem=send_sem,
        recv_sem=recv_sem,
        device_id=device,
        device_id_type=MESH,
    )


def columns(head):
    return pl.ds(pl.multiple_of(head * HD, HD), HD)


def place(chip, chips, step, sign):
    side = chips // 2
    turn = (step + 1) // 2
    far = (turn % 2) * ((turn + 1) // 2) + (1 - turn % 2) * (side - turn // 2)
    y = (chip % side + side + sign * (far % side)) % side
    x = (chip // side + (step + 1) % 2) % 2
    return x * side + y


def gather_kernel(
    chips,
    query_ref,
    key_ref,
    value_ref,
    query_out,
    key_out,
    value_out,
    query_send_sem,
    key_send_sem,
    value_send_sem,
    query_recv_sem,
    key_recv_sem,
    value_recv_sem,
    key_relay_send_sem,
    value_relay_send_sem,
    key_relay_recv_sem,
    value_relay_recv_sem,
    local_sem,
):
    seq = lax.axis_index("seq")
    chip = seq // 2
    core = seq % 2
    own_tile = seq
    partner = {"seq": 2 * chip + 1 - core}
    steps = chips - 1

    barrier = pltpu.get_barrier_semaphore()

    @pl.loop(1, chips)
    def _(k):
        other = {"seq": 2 * ((chip + k) % chips) + core}
        pl.semaphore_signal(barrier, inc=1, device_id=other, device_id_type=MESH)

    pl.semaphore_signal(barrier, inc=1, device_id=partner, device_id_type=MESH)

    own_key = pltpu.make_async_copy(
        key_ref.at[:, columns(chip)], key_out.at[own_tile], local_sem.at[0]
    )
    own_value = pltpu.make_async_copy(
        value_ref.at[:, columns(chip)], value_out.at[own_tile], local_sem.at[1]
    )
    own_query = pltpu.make_async_copy(
        query_ref.at[:, columns(chip)], query_out.at[chip], local_sem.at[2]
    )
    own_key.start()
    own_value.start()
    own_query.start()

    pl.semaphore_wait(barrier, chips)

    def shift(source, target, slot, send_sem, recv_sem, head):
        return remote(
            source.at[:, columns(head)],
            target.at[slot],
            send_sem.at[head],
            recv_sem.at[chip],
            {"seq": 2 * head + core},
        )

    def key_copy(head):
        return shift(key_ref, key_out, own_tile, key_send_sem, key_recv_sem, head)

    def value_copy(head):
        return shift(value_ref, value_out, own_tile, value_send_sem, value_recv_sem, head)

    def query_copy(head):
        return shift(query_ref, query_out, chip, query_send_sem, query_recv_sem, head)

    def relay(target, tile, send_sem, recv_sem):
        return remote(target.at[tile], target.at[tile], send_sem, recv_sem, partner)

    def key_relay(source):
        return relay(
            key_out,
            2 * source + core,
            key_relay_send_sem.at[source],
            key_relay_recv_sem.at[source],
        )

    def value_relay(source):
        return relay(
            value_out,
            2 * source + core,
            value_relay_send_sem.at[source],
            value_relay_recv_sem.at[source],
        )

    def arrived(buffer, slot, sem):
        remote(buffer.at[slot], buffer.at[slot], sem, sem, partner).wait_recv()

    @pl.loop(0, steps)
    def _(step):
        head = place(chip, chips, step, 1)
        key_copy(head).start()

    @pl.loop(0, steps)
    def _(step):
        head = place(chip, chips, step, 1)
        value_copy(head).start()

    @pl.loop(0, steps)
    def _(step):
        head = place(chip, chips, step, 1)
        query_copy(head).start()

    own_key.wait()
    key_relay(chip).start()
    own_value.wait()
    value_relay(chip).start()
    own_query.wait()

    @pl.loop(0, steps)
    def _(step):
        source = place(chip, chips, step, -1)
        arrived(key_out, 2 * source + core, key_recv_sem.at[source])
        key_relay(source).start()

    @pl.loop(0, steps)
    def _(step):
        source = place(chip, chips, step, -1)
        arrived(value_out, 2 * source + core, value_recv_sem.at[source])
        value_relay(source).start()

    @pl.loop(0, steps)
    def _(step):
        source = place(chip, chips, step, -1)
        arrived(query_out, source, query_recv_sem.at[source])
        head = place(chip, chips, step, 1)
        key_copy(head).wait_send()
        value_copy(head).wait_send()
        query_copy(head).wait_send()

    @pl.loop(0, chips)
    def _(source):
        tile = 2 * source + 1 - core
        arrived(key_out, tile, key_relay_recv_sem.at[source])
        arrived(value_out, tile, value_relay_recv_sem.at[source])
        key_relay(source).wait_send()
        value_relay(source).wait_send()


def attend_kernel(chips, most, clip_ref, query_ref, key_ref, value_ref, out_ref):
    core = lax.axis_index("seq") % 2
    tiles = 2 * chips

    def count(j, found):
        clip = clip_ref[0, j]
        return tuple(
            found[c] + jnp.where(clip < c + 1, 1, 0).astype(jnp.int32) for c in range(CLIPS - 1)
        )

    begins = lax.fori_loop(0, tiles, count, (jnp.int32(0),) * (CLIPS - 1))
    rate = LOG2E / math.sqrt(HD)
    ones = jnp.ones((CHUNK * TILE, HD), jnp.bfloat16)

    @pl.loop(0, chips)
    def _(source):
        clip = clip_ref[0, 2 * source + core]
        begin = jnp.int32(0)
        for c in range(1, CLIPS):
            begin = jnp.where(clip == c, begins[c - 1], begin)
        begin = jnp.minimum(begin, tiles - most)
        query = query_ref[source]
        scores = []
        top = None
        for j in range(most):
            score = lax.dot_general(
                query,
                key_ref[begin + j],
                (((1,), (1,)), ((), ())),
                preferred_element_type=jnp.float32,
            )
            score = score + jnp.where(clip_ref[0, begin + j] == clip, 0.0, -1e30)
            top = score if top is None else jnp.maximum(top, score)
            scores.append(score)
        top = jnp.max(top, axis=1, keepdims=True)
        summed = None
        for j in range(0, most, CHUNK):
            weights = jnp.concatenate(
                [jnp.exp2((scores[j + i] - top) * rate).astype(jnp.bfloat16) for i in range(CHUNK)],
                axis=1,
            )
            block = jnp.concatenate([value_ref[begin + j + i] for i in range(CHUNK)], axis=0)
            term = jnp.dot(
                weights,
                jnp.concatenate([block, ones], axis=1),
                preferred_element_type=jnp.float32,
            )
            summed = term if summed is None else summed + term
        out_ref[source] = summed[:, 0:HD] / summed[:, HD:]


def return_kernel(
    chips,
    clip_ref,
    attended_ref,
    gate_ref,
    out_ref,
    out_buf,
    land_buf,
    send_sem,
    recv_sem,
):
    seq = lax.axis_index("seq")
    chip = seq // 2
    core = seq % 2
    steps = chips - 1
    barrier = pltpu.get_barrier_semaphore()

    @pl.loop(1, chips)
    def _(k):
        other = {"seq": 2 * ((chip + k) % chips) + core}
        pl.semaphore_signal(barrier, inc=1, device_id=other, device_id_type=MESH)

    gates = gate_ref[...]

    def gated(source):
        clip = clip_ref[0, 2 * source + core]
        gate = gates[0:1, :]
        for c in range(1, CLIPS):
            gate = jnp.where(clip == c, gates[c : c + 1, :], gate)
        return (attended_ref[source] * gate).astype(jnp.bfloat16)

    @pl.loop(0, chips)
    def _(source):
        out_buf[source] = gated(source)

    pl.semaphore_wait(barrier, steps)

    def out_copy(other):
        return remote(
            out_buf.at[other],
            land_buf.at[chip],
            send_sem.at[other],
            recv_sem.at[chip],
            {"seq": 2 * other + core},
        )

    @pl.loop(0, steps)
    def _(step):
        other = place(chip, chips, step, -1)
        out_copy(other).start()

    out_ref[:, columns(chip)] = out_buf[chip]

    @pl.loop(0, steps)
    def _(step):
        other = place(chip, chips, step, -1)
        out_copy(other).wait_send()
        head = place(chip, chips, step, 1)
        remote(
            land_buf.at[head],
            land_buf.at[head],
            send_sem.at[head],
            recv_sem.at[head],
            {"seq": 2 * other + core},
        ).wait_recv()
        out_ref[:, columns(head)] = land_buf[head]


def per_device(query_rows, key_rows, value_rows, clip_tiles, conditioning, gate_weight):
    seq_count = lax.axis_size("seq")
    packs = lax.axis_size("dp")
    chips = seq_count // 2
    most = min(16, seq_count // 2)
    dma = pltpu.SemaphoreType.DMA
    vmem = pl.BlockSpec(memory_space=pltpu.VMEM)
    smem = pl.BlockSpec(memory_space=pltpu.SMEM)
    anywhere = pl.BlockSpec(memory_space=pl.ANY)

    act = jax.nn.silu(conditioning.astype(jnp.float32)).astype(jnp.bfloat16)
    part = jnp.dot(act, gate_weight, preferred_element_type=jnp.float32)
    parts = lax.all_to_all(part, "dp", split_axis=0, concat_axis=0, tiled=True)
    half = parts.reshape(packs, CLIPS, HD // 2).sum(axis=0)
    other_half = lax.ppermute(half, "seq", [(i, i ^ 1) for i in range(seq_count)])
    even = lax.axis_index("seq") % 2 == 0
    gates = jnp.concatenate(
        [jnp.where(even, half, other_half), jnp.where(even, other_half, half)], axis=1
    )

    query_all, key_all, value_all = pl.pallas_call(
        functools.partial(gather_kernel, chips),
        out_shape=[
            jax.ShapeDtypeStruct((chips, TILE, HD), jnp.bfloat16),
            jax.ShapeDtypeStruct((2 * chips, TILE, HD), jnp.bfloat16),
            jax.ShapeDtypeStruct((2 * chips, TILE, HD), jnp.bfloat16),
        ],
        in_specs=[anywhere] * 3,
        out_specs=[anywhere] * 3,
        scratch_shapes=[dma((chips,))] * 10 + [dma((3,))],
        compiler_params=pltpu.CompilerParams(
            collective_id=0, has_side_effects=True, vmem_limit_bytes=16 * 1024 * 1024
        ),
        cost_estimate=pl.CostEstimate(
            flops=0, bytes_accessed=200_000_000, transcendentals=0
        ),
        name="gather_heads",
    )(query_rows, key_rows, value_rows)

    attended = pl.pallas_call(
        functools.partial(attend_kernel, chips, most),
        out_shape=jax.ShapeDtypeStruct((chips, TILE, HD), jnp.float32),
        in_specs=[smem, vmem, vmem, vmem],
        out_specs=vmem,
        compiler_params=pltpu.CompilerParams(vmem_limit_bytes=40 * 1024 * 1024),
        cost_estimate=pl.CostEstimate(
            flops=4 * TILE * HD * TILE * most * chips,
            bytes_accessed=30_000_000,
            transcendentals=TILE * TILE * most * chips,
        ),
        name="attend",
    )(clip_tiles, query_all, key_all, value_all)

    return pl.pallas_call(
        functools.partial(return_kernel, chips),
        out_shape=jax.ShapeDtypeStruct(query_rows.shape, jnp.bfloat16),
        in_specs=[smem, vmem, vmem],
        out_specs=vmem,
        scratch_shapes=[
            pltpu.VMEM((chips, TILE, HD), jnp.bfloat16),
            pltpu.VMEM((chips, TILE, HD), jnp.bfloat16),
            dma((chips,)),
            dma((chips,)),
        ],
        compiler_params=pltpu.CompilerParams(
            collective_id=1, has_side_effects=True, vmem_limit_bytes=16 * 1024 * 1024
        ),
        name="return_tiles",
    )(clip_tiles, attended, gates)


def solution(mesh):
    return jax.shard_map(
        per_device,
        mesh=mesh,
        in_specs=(
            P(("dp", "seq"), None),
            P(("dp", "seq"), None),
            P(("dp", "seq"), None),
            P("dp", None),
            P(None, "dp"),
            P("dp", "seq"),
        ),
        out_specs=P(("dp", "seq"), None),
        check_vma=False,
    )
```

```python
import functools
import math

import jax
import jax.numpy as jnp
from jax import lax
from jax.experimental import pallas as pl
from jax.experimental.pallas import tpu as pltpu
from jax.sharding import PartitionSpec as P

HD = 128
TILE = 128
CLIPS = 4
CHUNK = 2
GROUP = 4
ATTEND_VMEM = 60
LOG2E = 1.4426950408889634
MESH = pl.DeviceIdType.MESH


def remote(src, dst, send_sem, recv_sem, device):
    return pltpu.make_async_remote_copy(
        src_ref=src,
        dst_ref=dst,
        send_sem=send_sem,
        recv_sem=recv_sem,
        device_id=device,
        device_id_type=MESH,
    )


def columns(head):
    return pl.ds(pl.multiple_of(head * HD, HD), HD)


def place(chip, chips, step, sign):
    side = chips // 2
    turn = (step + 1) // 2
    far = (turn % 2) * ((turn + 1) // 2) + (1 - turn % 2) * (side - turn // 2)
    y = (chip % side + side + sign * (far % side)) % side
    x = (chip // side + (step + 1) % 2) % 2
    return x * side + y


def gather_kernel(
    chips,
    query_ref,
    key_ref,
    value_ref,
    query_out,
    key_out,
    value_out,
    query_send_sem,
    key_send_sem,
    value_send_sem,
    query_recv_sem,
    key_recv_sem,
    value_recv_sem,
    key_relay_send_sem,
    value_relay_send_sem,
    key_relay_recv_sem,
    value_relay_recv_sem,
    local_sem,
):
    seq = lax.axis_index("seq")
    chip = seq // 2
    core = seq % 2
    own_tile = seq
    partner = {"seq": 2 * chip + 1 - core}
    steps = chips - 1

    barrier = pltpu.get_barrier_semaphore()

    @pl.loop(1, chips)
    def _(k):
        other = {"seq": 2 * ((chip + k) % chips) + core}
        pl.semaphore_signal(barrier, inc=1, device_id=other, device_id_type=MESH)

    pl.semaphore_signal(barrier, inc=1, device_id=partner, device_id_type=MESH)

    own_key = pltpu.make_async_copy(
        key_ref.at[:, columns(chip)], key_out.at[own_tile], local_sem.at[0]
    )
    own_value = pltpu.make_async_copy(
        value_ref.at[:, columns(chip)], value_out.at[own_tile], local_sem.at[1]
    )
    own_query = pltpu.make_async_copy(
        query_ref.at[:, columns(chip)], query_out.at[chip], local_sem.at[2]
    )
    own_key.start()
    own_value.start()
    own_query.start()

    pl.semaphore_wait(barrier, chips)

    def shift(source, target, slot, send_sem, recv_sem, head):
        return remote(
            source.at[:, columns(head)],
            target.at[slot],
            send_sem.at[head],
            recv_sem.at[chip],
            {"seq": 2 * head + core},
        )

    def key_copy(head):
        return shift(key_ref, key_out, own_tile, key_send_sem, key_recv_sem, head)

    def value_copy(head):
        return shift(value_ref, value_out, own_tile, value_send_sem, value_recv_sem, head)

    def query_copy(head):
        return shift(query_ref, query_out, chip, query_send_sem, query_recv_sem, head)

    def relay(target, tile, send_sem, recv_sem):
        return remote(target.at[tile], target.at[tile], send_sem, recv_sem, partner)

    def key_relay(source):
        return relay(
            key_out,
            2 * source + core,
            key_relay_send_sem.at[source],
            key_relay_recv_sem.at[source],
        )

    def value_relay(source):
        return relay(
            value_out,
            2 * source + core,
            value_relay_send_sem.at[source],
            value_relay_recv_sem.at[source],
        )

    def arrived(buffer, slot, sem):
        remote(buffer.at[slot], buffer.at[slot], sem, sem, partner).wait_recv()

    @pl.loop(0, steps)
    def _(step):
        head = place(chip, chips, step, 1)
        key_copy(head).start()

    @pl.loop(0, steps)
    def _(step):
        head = place(chip, chips, step, 1)
        value_copy(head).start()

    @pl.loop(0, steps)
    def _(step):
        head = place(chip, chips, step, 1)
        query_copy(head).start()

    own_key.wait()
    key_relay(chip).start()
    own_value.wait()
    value_relay(chip).start()
    own_query.wait()

    @pl.loop(0, steps)
    def _(step):
        source = place(chip, chips, step, -1)
        arrived(key_out, 2 * source + core, key_recv_sem.at[source])
        key_relay(source).start()

    @pl.loop(0, steps)
    def _(step):
        source = place(chip, chips, step, -1)
        arrived(value_out, 2 * source + core, value_recv_sem.at[source])
        value_relay(source).start()

    @pl.loop(0, steps)
    def _(step):
        source = place(chip, chips, step, -1)
        arrived(query_out, source, query_recv_sem.at[source])
        head = place(chip, chips, step, 1)
        key_copy(head).wait_send()
        value_copy(head).wait_send()
        query_copy(head).wait_send()

    @pl.loop(0, chips)
    def _(source):
        tile = 2 * source + 1 - core
        arrived(key_out, tile, key_relay_recv_sem.at[source])
        arrived(value_out, tile, value_relay_recv_sem.at[source])
        key_relay(source).wait_send()
        value_relay(source).wait_send()


def gate_kernel(packs, cond_ref, weight_ref, half_ref, send_buf, recv_buf, send_sem, recv_sem):
    pack = lax.axis_index("dp")
    barrier = pltpu.get_barrier_semaphore()

    @pl.loop(1, packs)
    def _(k):
        other = {"dp": (pack + k) % packs}
        pl.semaphore_signal(barrier, inc=1, device_id=other, device_id_type=MESH)

    cond = cond_ref[...].astype(jnp.float32)
    act = (cond / (1.0 + jnp.exp(-cond))).astype(jnp.bfloat16)
    part = jnp.dot(act, weight_ref[...], preferred_element_type=jnp.float32)
    send_buf[...] = jnp.zeros_like(send_buf)
    for p in range(packs):
        send_buf[p, 0:CLIPS, 0 : HD // 2] = part[p * CLIPS : (p + 1) * CLIPS, :]
    recv_buf[pack] = send_buf[pack]

    pl.semaphore_wait(barrier, packs - 1)

    def gate_copy(other):
        return remote(
            send_buf.at[other],
            recv_buf.at[pack],
            send_sem.at[other],
            recv_sem.at[pack],
            {"dp": other},
        )

    @pl.loop(1, packs)
    def _(k):
        gate_copy((pack + k) % packs).start()

    @pl.loop(1, packs)
    def _(k):
        source = (pack + packs - k) % packs
        remote(
            recv_buf.at[source],
            recv_buf.at[source],
            send_sem.at[source],
            recv_sem.at[source],
            {"dp": source},
        ).wait_recv()

    half_ref[...] = jnp.sum(recv_buf[...], axis=0)

    @pl.loop(1, packs)
    def _(k):
        gate_copy((pack + k) % packs).wait_send()


def attend_kernel(
    chips,
    most,
    clip_ref,
    query_buf,
    key_buf,
    value_buf,
    half_ref,
    other_ref,
    out_ref,
):
    seq = lax.axis_index("seq")
    core = seq % 2
    tiles = 2 * chips
    def count(j, found):
        clip = clip_ref[0, j]
        return tuple(
            found[c] + jnp.where(clip < c + 1, 1, 0).astype(jnp.int32) for c in range(CLIPS - 1)
        )

    begins = lax.fori_loop(0, tiles, count, (jnp.int32(0),) * (CLIPS - 1))
    rate = LOG2E / math.sqrt(HD)
    ones = jnp.ones((CHUNK * TILE, HD), jnp.bfloat16)

    half = half_ref[:, 0 : HD // 2]
    other_half = other_ref[:, 0 : HD // 2]
    gates = jnp.where(
        core == 0,
        jnp.concatenate([half, other_half], axis=1),
        jnp.concatenate([other_half, half], axis=1),
    )

    def weigh(source):
        clip = clip_ref[0, 2 * source + core]
        begin = jnp.int32(0)
        gate = gates[0:1, :]
        for c in range(1, CLIPS):
            begin = jnp.where(clip == c, begins[c - 1], begin)
            gate = jnp.where(clip == c, gates[c : c + 1, :], gate)
        begin = jnp.minimum(begin, tiles - most)
        query = query_buf[source]
        scores = []
        for j in range(0, most, CHUNK):
            block = jnp.concatenate([key_buf[begin + j + i] for i in range(CHUNK)], axis=0)
            score = lax.dot_general(
                query, block, (((1,), (1,)), ((), ())), preferred_element_type=jnp.float32
            )
            for i in range(CHUNK):
                hide = jnp.where(clip_ref[0, begin + j + i] == clip, 0.0, -1e30)
                scores.append(score[:, i * TILE : (i + 1) * TILE] + hide)
        tops = scores
        while len(tops) > 1:
            tops = [jnp.maximum(a, b) for a, b in zip(tops[0::2], tops[1::2])]
        return begin, gate, scores, jnp.max(tops[0], axis=1, keepdims=True)

    def mix(slot, begin, gate, scores, top):
        summed = None
        for j in range(0, most, CHUNK):
            weights = jnp.concatenate(
                [jnp.exp2((scores[j + i] - top) * rate).astype(jnp.bfloat16) for i in range(CHUNK)],
                axis=1,
            )
            block = jnp.concatenate([value_buf[begin + j + i] for i in range(CHUNK)], axis=0)
            term = jnp.dot(
                weights,
                jnp.concatenate([block, ones], axis=1),
                preferred_element_type=jnp.float32,
            )
            summed = term if summed is None else summed + term
        out_ref[slot] = (summed[:, 0:HD] / summed[:, HD:] * gate).astype(jnp.bfloat16)

    @pl.loop(0, chips // GROUP)
    def _(group):
        slots = [group * GROUP + i for i in range(GROUP)]
        states = [weigh(slot) for slot in slots]
        for slot, state in zip(slots, states):
            mix(slot, *state)


def return_kernel(chips, attended_ref, out_ref, land_buf, send_sem, recv_sem, local_sem):
    seq = lax.axis_index("seq")
    chip = seq // 2
    core = seq % 2
    partner = {"seq": 2 * chip + 1 - core}
    steps = chips - 1
    barrier = pltpu.get_barrier_semaphore()

    @pl.loop(1, chips)
    def _(k):
        other = {"seq": 2 * ((chip + k) % chips) + core}
        pl.semaphore_signal(barrier, inc=1, device_id=other, device_id_type=MESH)

    own = pltpu.make_async_copy(attended_ref.at[chip], land_buf.at[chip], local_sem)
    own.start()

    pl.semaphore_wait(barrier, steps)

    def out_copy(other):
        return remote(
            attended_ref.at[other],
            land_buf.at[chip],
            send_sem.at[other],
            recv_sem.at[chip],
            {"seq": 2 * other + core},
        )

    @pl.loop(0, steps)
    def _(step):
        out_copy(place(chip, chips, chips - 2 - step, -1)).start()

    own.wait()
    out_ref[:, columns(chip)] = land_buf[chip]

    @pl.loop(0, steps)
    def _(step):
        head = place(chip, chips, chips - 2 - step, 1)
        remote(
            land_buf.at[head],
            land_buf.at[head],
            send_sem.at[head],
            recv_sem.at[head],
            partner,
        ).wait_recv()
        out_ref[:, columns(head)] = land_buf[head]

    @pl.loop(0, steps)
    def _(step):
        out_copy(place(chip, chips, step, -1)).wait_send()


def per_device(query_rows, key_rows, value_rows, clip_tiles, conditioning, gate_weight):
    seq_count = lax.axis_size("seq")
    packs = lax.axis_size("dp")
    chips = seq_count // 2
    most = min(16, seq_count // 2)
    dma = pltpu.SemaphoreType.DMA
    vmem = pl.BlockSpec(memory_space=pltpu.VMEM)
    smem = pl.BlockSpec(memory_space=pltpu.SMEM)
    anywhere = pl.BlockSpec(memory_space=pl.ANY)
    part_shape = jax.ShapeDtypeStruct((chips, TILE, HD), jnp.bfloat16)
    whole_shape = jax.ShapeDtypeStruct((2 * chips, TILE, HD), jnp.bfloat16)

    half = pl.pallas_call(
        functools.partial(gate_kernel, packs),
        out_shape=jax.ShapeDtypeStruct((8, HD), jnp.float32),
        in_specs=[vmem, vmem],
        out_specs=vmem,
        scratch_shapes=[
            pltpu.VMEM((packs, 8, HD), jnp.float32),
            pltpu.VMEM((packs, 8, HD), jnp.float32),
            dma((packs,)),
            dma((packs,)),
        ],
        compiler_params=pltpu.CompilerParams(collective_id=2, has_side_effects=True),
        name="sum_gates",
    )(conditioning, gate_weight)

    other = lax.ppermute(half, "seq", [(i, i ^ 1) for i in range(seq_count)])

    query_all, key_all, value_all = pl.pallas_call(
        functools.partial(gather_kernel, chips),
        out_shape=[part_shape, whole_shape, whole_shape],
        in_specs=[anywhere] * 3,
        out_specs=[anywhere] * 3,
        scratch_shapes=[dma((chips,))] * 10 + [dma((3,))],
        compiler_params=pltpu.CompilerParams(collective_id=0, has_side_effects=True),
        name="gather_heads",
    )(query_rows, key_rows, value_rows)

    attended = pl.pallas_call(
        functools.partial(attend_kernel, chips, most),
        out_shape=part_shape,
        in_specs=[smem, vmem, vmem, vmem, vmem, vmem],
        out_specs=vmem,
        compiler_params=pltpu.CompilerParams(vmem_limit_bytes=ATTEND_VMEM * 1024 * 1024),
        name="attend",
    )(clip_tiles, query_all, key_all, value_all, half, other)

    return pl.pallas_call(
        functools.partial(return_kernel, chips),
        out_shape=jax.ShapeDtypeStruct(query_rows.shape, jnp.bfloat16),
        in_specs=[anywhere],
        out_specs=vmem,
        scratch_shapes=[
            pltpu.VMEM((chips, TILE, HD), jnp.bfloat16),
            dma((chips,)),
            dma((chips,)),
            dma,
        ],
        compiler_params=pltpu.CompilerParams(collective_id=1, has_side_effects=True),
        name="return_tiles",
    )(attended)


def solution(mesh):
    return jax.shard_map(
        per_device,
        mesh=mesh,
        in_specs=(
            P(("dp", "seq"), None),
            P(("dp", "seq"), None),
            P(("dp", "seq"), None),
            P("dp", None),
            P(None, "dp"),
            P("dp", "seq"),
        ),
        out_specs=P(("dp", "seq"), None),
        check_vma=False,
    )
```

```python
import functools
import math

import jax
import jax.numpy as jnp
from jax import lax
from jax.experimental import pallas as pl
from jax.experimental.pallas import tpu as pltpu
from jax.sharding import PartitionSpec as P

HD = 128
TILE = 128
CLIPS = 4
CHUNK = 2
GROUP = 4
ATTEND_VMEM = 60
LOG2E = 1.4426950408889634
MESH = pl.DeviceIdType.MESH


def remote(src, dst, send_sem, recv_sem, device):
    return pltpu.make_async_remote_copy(
        src_ref=src,
        dst_ref=dst,
        send_sem=send_sem,
        recv_sem=recv_sem,
        device_id=device,
        device_id_type=MESH,
    )


def columns(head):
    return pl.ds(pl.multiple_of(head * HD, HD), HD)


def others(chip, chips, sign):
    side = chips // 2
    x, y = lax.div(chip, side), lax.rem(chip, side)
    found = []
    for turn in range(side):
        far = (turn + 1) // 2 if turn % 2 else (side - turn // 2) % side
        row = lax.rem(y + (far if sign > 0 else side - far), side)
        for cross in range(2):
            if turn or cross:
                found.append(lax.rem(x + cross, 2) * side + row)
    return found


def gather_kernel(
    chips,
    packs,
    query_ref,
    key_ref,
    value_ref,
    cond_ref,
    weight_ref,
    query_out,
    key_out,
    value_out,
    gate_out,
    gate_send,
    gate_recv,
    gate_half,
    query_send_sem,
    key_send_sem,
    value_send_sem,
    query_recv_sem,
    key_recv_sem,
    value_recv_sem,
    key_relay_send_sem,
    value_relay_send_sem,
    key_relay_recv_sem,
    value_relay_recv_sem,
    local_sem,
    gate_send_sem,
    gate_recv_sem,
    half_send_sem,
    half_recv_sem,
):
    pack = lax.axis_index("dp")
    seq = lax.axis_index("seq")
    chip = lax.div(seq, 2)
    core = lax.rem(seq, 2)
    own_tile = seq
    partner = {"seq": 2 * chip + 1 - core}
    ahead = others(chip, chips, 1)
    behind = others(chip, chips, -1)
    packs_ahead = [lax.rem(pack + k, packs) for k in range(1, packs)]

    barrier = pltpu.get_barrier_semaphore()

    for head in ahead:
        other = {"seq": 2 * head + core}
        pl.semaphore_signal(barrier, inc=1, device_id=other, device_id_type=MESH)

    pl.semaphore_signal(barrier, inc=1, device_id=partner, device_id_type=MESH)
    for other in packs_ahead:
        pl.semaphore_signal(barrier, inc=1, device_id={"dp": other}, device_id_type=MESH)

    own_key = pltpu.make_async_copy(
        key_ref.at[:, columns(chip)], key_out.at[own_tile], local_sem.at[0]
    )
    own_value = pltpu.make_async_copy(
        value_ref.at[:, columns(chip)], value_out.at[own_tile], local_sem.at[1]
    )
    own_query = pltpu.make_async_copy(
        query_ref.at[:, columns(chip)], query_out.at[chip], local_sem.at[2]
    )
    own_key.start()
    own_value.start()
    own_query.start()

    cond = cond_ref[...].astype(jnp.float32)
    act = (cond / (1.0 + jnp.exp(-cond))).astype(jnp.bfloat16)
    part = lax.dot_general(
        act, weight_ref[...], (((1,), (1,)), ((), ())), preferred_element_type=jnp.float32
    )
    gate_send[...] = jnp.zeros_like(gate_send)
    for p in range(packs):
        gate_send[p, 0:CLIPS, 0 : HD // 2] = part[p * CLIPS : (p + 1) * CLIPS, :]
    gate_recv[pack] = gate_send[pack]

    pl.semaphore_wait(barrier, chips + packs - 1)

    def shift(source, target, slot, send_sem, recv_sem, head):
        return remote(
            source.at[:, columns(head)],
            target.at[slot],
            send_sem.at[head],
            recv_sem.at[chip],
            {"seq": 2 * head + core},
        )

    def key_copy(head):
        return shift(key_ref, key_out, own_tile, key_send_sem, key_recv_sem, head)

    def value_copy(head):
        return shift(value_ref, value_out, own_tile, value_send_sem, value_recv_sem, head)

    def query_copy(head):
        return shift(query_ref, query_out, chip, query_send_sem, query_recv_sem, head)

    def relay(target, tile, send_sem, recv_sem):
        return remote(target.at[tile], target.at[tile], send_sem, recv_sem, partner)

    def key_relay(source):
        return relay(
            key_out,
            2 * source + core,
            key_relay_send_sem.at[source],
            key_relay_recv_sem.at[source],
        )

    def value_relay(source):
        return relay(
            value_out,
            2 * source + core,
            value_relay_send_sem.at[source],
            value_relay_recv_sem.at[source],
        )

    def arrived(buffer, slot, sem):
        remote(buffer.at[slot], buffer.at[slot], sem, sem, partner).wait_recv()

    def gate_copy(other):
        return remote(
            gate_send.at[other],
            gate_recv.at[pack],
            gate_send_sem.at[other],
            gate_recv_sem.at[pack],
            {"dp": other},
        )

    for head in ahead:
        key_copy(head).start()
    own_key.wait()
    key_relay(chip).start()
    for head in ahead:
        value_copy(head).start()
    own_value.wait()
    value_relay(chip).start()
    for head in ahead:
        query_copy(head).start()
    for other in packs_ahead:
        gate_copy(other).start()

    for source in behind:
        arrived(key_out, 2 * source + core, key_recv_sem.at[source])
        key_relay(source).start()

    for source in packs_ahead:
        arrived(gate_recv, source, gate_recv_sem.at[source])
    gate_half[core] = jnp.sum(gate_recv[...], axis=0)
    half_copy = remote(
        gate_half.at[core], gate_half.at[core], half_send_sem, half_recv_sem, partner
    )
    half_copy.start()

    for source in behind:
        arrived(value_out, 2 * source + core, value_recv_sem.at[source])
        value_relay(source).start()

    arrived(gate_half, 1 - core, half_recv_sem)
    gate_out[...] = jnp.concatenate(
        [gate_half[0, :, 0 : HD // 2], gate_half[1, :, 0 : HD // 2]], axis=1
    )
    half_copy.wait_send()
    for other in packs_ahead:
        gate_copy(other).wait_send()

    own_query.wait()
    for head in ahead:
        key_copy(head).wait_send()
        value_copy(head).wait_send()
        query_copy(head).wait_send()
    for source in behind:
        arrived(query_out, source, query_recv_sem.at[source])

    for source in behind + [chip]:
        tile = 2 * source + 1 - core
        arrived(key_out, tile, key_relay_recv_sem.at[source])
        arrived(value_out, tile, value_relay_recv_sem.at[source])
        key_relay(source).wait_send()
        value_relay(source).wait_send()


def attend_kernel(
    chips,
    most,
    clip_ref,
    query_buf,
    key_buf,
    value_buf,
    gate_ref,
    out_ref,
):
    seq = lax.axis_index("seq")
    core = seq % 2
    tiles = 2 * chips
    def count(j, found):
        clip = clip_ref[0, j]
        return tuple(
            found[c] + jnp.where(clip < c + 1, 1, 0).astype(jnp.int32) for c in range(CLIPS - 1)
        )

    begins = lax.fori_loop(0, tiles, count, (jnp.int32(0),) * (CLIPS - 1))
    rate = LOG2E / math.sqrt(HD)
    ones = jnp.ones((CHUNK * TILE, HD), jnp.bfloat16)

    gates = gate_ref[...]

    def weigh(source):
        clip = clip_ref[0, 2 * source + core]
        begin = jnp.int32(0)
        gate = gates[0:1, :]
        for c in range(1, CLIPS):
            begin = jnp.where(clip == c, begins[c - 1], begin)
            gate = jnp.where(clip == c, gates[c : c + 1, :], gate)
        begin = jnp.minimum(begin, tiles - most)
        query = query_buf[source]
        scores = []
        for j in range(0, most, CHUNK):
            block = jnp.concatenate([key_buf[begin + j + i] for i in range(CHUNK)], axis=0)
            score = lax.dot_general(
                query, block, (((1,), (1,)), ((), ())), preferred_element_type=jnp.float32
            )
            for i in range(CHUNK):
                hide = jnp.where(clip_ref[0, begin + j + i] == clip, 0.0, -1e30)
                scores.append(score[:, i * TILE : (i + 1) * TILE] + hide)
        tops = scores
        while len(tops) > 1:
            tops = [jnp.maximum(a, b) for a, b in zip(tops[0::2], tops[1::2])]
        return begin, gate, scores, jnp.max(tops[0], axis=1, keepdims=True)

    def mix(slot, begin, gate, scores, top):
        summed = None
        for j in range(0, most, CHUNK):
            weights = jnp.concatenate(
                [jnp.exp2((scores[j + i] - top) * rate).astype(jnp.bfloat16) for i in range(CHUNK)],
                axis=1,
            )
            block = jnp.concatenate([value_buf[begin + j + i] for i in range(CHUNK)], axis=0)
            term = jnp.dot(
                weights,
                jnp.concatenate([block, ones], axis=1),
                preferred_element_type=jnp.float32,
            )
            summed = term if summed is None else summed + term
        out_ref[slot] = (summed[:, 0:HD] / summed[:, HD:] * gate).astype(jnp.bfloat16)

    @pl.loop(0, chips // GROUP)
    def _(group):
        slots = [group * GROUP + i for i in range(GROUP)]
        states = [weigh(slot) for slot in slots]
        for slot, state in zip(slots, states):
            mix(slot, *state)


def return_kernel(chips, attended_ref, out_ref, land_buf, send_sem, recv_sem, local_sem):
    seq = lax.axis_index("seq")
    chip = lax.div(seq, 2)
    core = lax.rem(seq, 2)
    partner = {"seq": 2 * chip + 1 - core}
    ahead = others(chip, chips, 1)[::-1]
    behind = others(chip, chips, -1)[::-1]
    barrier = pltpu.get_barrier_semaphore()

    for other in behind:
        device = {"seq": 2 * other + core}
        pl.semaphore_signal(barrier, inc=1, device_id=device, device_id_type=MESH)

    own = pltpu.make_async_copy(attended_ref.at[chip], land_buf.at[chip], local_sem)
    own.start()

    pl.semaphore_wait(barrier, chips - 1)

    def out_copy(other):
        return remote(
            attended_ref.at[other],
            land_buf.at[chip],
            send_sem.at[other],
            recv_sem.at[chip],
            {"seq": 2 * other + core},
        )

    for other in behind:
        out_copy(other).start()

    own.wait()
    out_ref[:, columns(chip)] = land_buf[chip]

    for head in ahead:
        remote(
            land_buf.at[head], land_buf.at[head], send_sem.at[head], recv_sem.at[head], partner
        ).wait_recv()
        out_ref[:, columns(head)] = land_buf[head]

    for other in behind:
        out_copy(other).wait_send()


def per_device(query_rows, key_rows, value_rows, clip_tiles, conditioning, gate_weight):
    seq_count = lax.axis_size("seq")
    packs = lax.axis_size("dp")
    chips = seq_count // 2
    most = min(16, seq_count // 2)
    dma = pltpu.SemaphoreType.DMA
    vmem = pl.BlockSpec(memory_space=pltpu.VMEM)
    smem = pl.BlockSpec(memory_space=pltpu.SMEM)
    anywhere = pl.BlockSpec(memory_space=pl.ANY)
    part_shape = jax.ShapeDtypeStruct((chips, TILE, HD), jnp.bfloat16)
    whole_shape = jax.ShapeDtypeStruct((2 * chips, TILE, HD), jnp.bfloat16)

    gate_buf = pltpu.VMEM((packs, 8, HD), jnp.float32)
    query_all, key_all, value_all, gates = pl.pallas_call(
        functools.partial(gather_kernel, chips, packs),
        out_shape=[
            part_shape,
            whole_shape,
            whole_shape,
            jax.ShapeDtypeStruct((8, HD), jnp.float32),
        ],
        in_specs=[anywhere] * 3 + [vmem] * 2,
        out_specs=[anywhere] * 3 + [vmem],
        scratch_shapes=[gate_buf, gate_buf, pltpu.VMEM((2, 8, HD), jnp.float32)]
        + [dma((chips,))] * 10
        + [dma((3,)), dma((packs,)), dma((packs,)), dma, dma],
        compiler_params=pltpu.CompilerParams(collective_id=0, has_side_effects=True),
        name="gather_heads",
    )(query_rows, key_rows, value_rows, conditioning, gate_weight.T)

    attended = pl.pallas_call(
        functools.partial(attend_kernel, chips, most),
        out_shape=part_shape,
        in_specs=[smem, vmem, vmem, vmem, vmem],
        out_specs=vmem,
        compiler_params=pltpu.CompilerParams(vmem_limit_bytes=ATTEND_VMEM * 1024 * 1024),
        name="attend",
    )(clip_tiles, query_all, key_all, value_all, gates)

    return pl.pallas_call(
        functools.partial(return_kernel, chips),
        out_shape=jax.ShapeDtypeStruct(query_rows.shape, jnp.bfloat16),
        in_specs=[anywhere],
        out_specs=vmem,
        scratch_shapes=[
            pltpu.VMEM((chips, TILE, HD), jnp.bfloat16),
            dma((chips,)),
            dma((chips,)),
            dma,
        ],
        compiler_params=pltpu.CompilerParams(collective_id=1, has_side_effects=True),
        name="return_tiles",
    )(attended)


def solution(mesh):
    return jax.shard_map(
        per_device,
        mesh=mesh,
        in_specs=(
            P(("dp", "seq"), None),
            P(("dp", "seq"), None),
            P(("dp", "seq"), None),
            P("dp", None),
            P(None, "dp"),
            P("dp", "seq"),
        ),
        out_specs=P(("dp", "seq"), None),
        check_vma=False,
    )
```

```python
import functools
import math

import jax
import jax.numpy as jnp
from jax import lax
from jax.experimental import pallas as pl
from jax.experimental.pallas import tpu as pltpu
from jax.sharding import PartitionSpec as P

HD = 128
TILE = 128
CLIPS = 4
CHUNK = 2
GROUP = 8
ATTEND_VMEM = 60
LOG2E = 1.4426950408889634
MESH = pl.DeviceIdType.MESH


def remote(src, dst, send_sem, recv_sem, device):
    return pltpu.make_async_remote_copy(
        src_ref=src,
        dst_ref=dst,
        send_sem=send_sem,
        recv_sem=recv_sem,
        device_id=device,
        device_id_type=MESH,
    )


def columns(head):
    return pl.ds(pl.multiple_of(head * HD, HD), HD)


def others(chip, chips, sign):
    side = chips // 2
    x, y = lax.div(chip, side), lax.rem(chip, side)
    found = []
    for turn in range(side):
        far = (turn + 1) // 2 if turn % 2 else (side - turn // 2) % side
        row = lax.rem(y + (far if sign > 0 else side - far), side)
        for cross in range(2):
            if turn or cross:
                found.append(lax.rem(x + cross, 2) * side + row)
    return found


def gather_kernel(
    chips,
    packs,
    query_ref,
    key_ref,
    value_ref,
    cond_ref,
    weight_ref,
    query_out,
    key_out,
    value_out,
    gate_out,
    gate_send,
    gate_recv,
    gate_half,
    query_send_sem,
    key_send_sem,
    value_send_sem,
    query_recv_sem,
    key_recv_sem,
    value_recv_sem,
    key_relay_send_sem,
    value_relay_send_sem,
    key_relay_recv_sem,
    value_relay_recv_sem,
    local_sem,
    gate_send_sem,
    gate_recv_sem,
    half_send_sem,
    half_recv_sem,
):
    pack = lax.axis_index("dp")
    seq = lax.axis_index("seq")
    chip = lax.div(seq, 2)
    core = lax.rem(seq, 2)
    own_tile = seq
    partner = {"seq": 2 * chip + 1 - core}
    ahead = others(chip, chips, 1)[::-1]
    behind = others(chip, chips, -1)[::-1]
    packs_ahead = [lax.rem(pack + k, packs) for k in range(1, packs)]

    barrier = pltpu.get_barrier_semaphore()

    for head in ahead:
        other = {"seq": 2 * head + core}
        pl.semaphore_signal(barrier, inc=1, device_id=other, device_id_type=MESH)

    pl.semaphore_signal(barrier, inc=1, device_id=partner, device_id_type=MESH)
    for other in packs_ahead:
        pl.semaphore_signal(barrier, inc=1, device_id={"dp": other}, device_id_type=MESH)

    own_key = pltpu.make_async_copy(
        key_ref.at[:, columns(chip)], key_out.at[own_tile], local_sem.at[0]
    )
    own_value = pltpu.make_async_copy(
        value_ref.at[:, columns(chip)], value_out.at[own_tile], local_sem.at[1]
    )
    own_query = pltpu.make_async_copy(
        query_ref.at[:, columns(chip)], query_out.at[chip], local_sem.at[2]
    )
    own_key.start()
    own_value.start()
    own_query.start()

    cond = cond_ref[...].astype(jnp.float32)
    act = (cond / (1.0 + jnp.exp(-cond))).astype(jnp.bfloat16)
    part = lax.dot_general(
        act, weight_ref[...], (((1,), (1,)), ((), ())), preferred_element_type=jnp.float32
    )
    gate_send[...] = jnp.zeros_like(gate_send)
    for p in range(packs):
        gate_send[p, 0:CLIPS, 0 : HD // 2] = part[p * CLIPS : (p + 1) * CLIPS, :]
    gate_recv[pack] = gate_send[pack]

    pl.semaphore_wait(barrier, chips + packs - 1)

    def shift(source, target, slot, send_sem, recv_sem, head):
        return remote(
            source.at[:, columns(head)],
            target.at[slot],
            send_sem.at[head],
            recv_sem.at[chip],
            {"seq": 2 * head + core},
        )

    def key_copy(head):
        return shift(key_ref, key_out, own_tile, key_send_sem, key_recv_sem, head)

    def value_copy(head):
        return shift(value_ref, value_out, own_tile, value_send_sem, value_recv_sem, head)

    def query_copy(head):
        return shift(query_ref, query_out, chip, query_send_sem, query_recv_sem, head)

    def relay(target, tile, send_sem, recv_sem):
        return remote(target.at[tile], target.at[tile], send_sem, recv_sem, partner)

    def key_relay(source):
        return relay(
            key_out,
            2 * source + core,
            key_relay_send_sem.at[source],
            key_relay_recv_sem.at[source],
        )

    def value_relay(source):
        return relay(
            value_out,
            2 * source + core,
            value_relay_send_sem.at[source],
            value_relay_recv_sem.at[source],
        )

    def arrived(buffer, slot, sem):
        remote(buffer.at[slot], buffer.at[slot], sem, sem, partner).wait_recv()

    def gate_copy(other):
        return remote(
            gate_send.at[other],
            gate_recv.at[pack],
            gate_send_sem.at[other],
            gate_recv_sem.at[pack],
            {"dp": other},
        )

    for head in ahead:
        key_copy(head).start()
    own_key.wait()
    key_relay(chip).start()
    for head in ahead:
        value_copy(head).start()
    own_value.wait()
    value_relay(chip).start()
    for head in ahead:
        query_copy(head).start()
    for other in packs_ahead:
        gate_copy(other).start()

    for source in behind:
        arrived(key_out, 2 * source + core, key_recv_sem.at[source])
        key_relay(source).start()

    for source in packs_ahead:
        arrived(gate_recv, source, gate_recv_sem.at[source])
    gate_half[core] = jnp.sum(gate_recv[...], axis=0)
    half_copy = remote(
        gate_half.at[core], gate_half.at[core], half_send_sem, half_recv_sem, partner
    )
    half_copy.start()

    for source in behind:
        arrived(value_out, 2 * source + core, value_recv_sem.at[source])
        value_relay(source).start()

    arrived(gate_half, 1 - core, half_recv_sem)
    gate_out[...] = jnp.concatenate(
        [gate_half[0, :, 0 : HD // 2], gate_half[1, :, 0 : HD // 2]], axis=1
    )
    half_copy.wait_send()
    for other in packs_ahead:
        gate_copy(other).wait_send()

    own_query.wait()
    for head in ahead:
        key_copy(head).wait_send()
        value_copy(head).wait_send()
        query_copy(head).wait_send()
    for source in behind:
        arrived(query_out, source, query_recv_sem.at[source])

    for source in behind + [chip]:
        tile = 2 * source + 1 - core
        arrived(key_out, tile, key_relay_recv_sem.at[source])
        arrived(value_out, tile, value_relay_recv_sem.at[source])
        key_relay(source).wait_send()
        value_relay(source).wait_send()


def attend_kernel(
    chips,
    most,
    clip_ref,
    query_buf,
    key_buf,
    value_buf,
    gate_ref,
    out_ref,
):
    seq = lax.axis_index("seq")
    core = seq % 2
    tiles = 2 * chips
    def count(j, found):
        clip = clip_ref[0, j]
        return tuple(
            found[c] + jnp.where(clip < c + 1, 1, 0).astype(jnp.int32) for c in range(CLIPS - 1)
        )

    begins = lax.fori_loop(0, tiles, count, (jnp.int32(0),) * (CLIPS - 1))
    rate = LOG2E / math.sqrt(HD)
    ones = jnp.ones((CHUNK * TILE, HD), jnp.bfloat16)

    gates = gate_ref[...]

    def weigh(source):
        clip = clip_ref[0, 2 * source + core]
        begin = jnp.int32(0)
        gate = gates[0:1, :]
        for c in range(1, CLIPS):
            begin = jnp.where(clip == c, begins[c - 1], begin)
            gate = jnp.where(clip == c, gates[c : c + 1, :], gate)
        begin = jnp.minimum(begin, tiles - most)
        query = query_buf[source]
        scores = []
        for j in range(0, most, CHUNK):
            block = jnp.concatenate([key_buf[begin + j + i] for i in range(CHUNK)], axis=0)
            score = lax.dot_general(
                query, block, (((1,), (1,)), ((), ())), preferred_element_type=jnp.float32
            )
            for i in range(CHUNK):
                hide = jnp.where(clip_ref[0, begin + j + i] == clip, 0.0, -1e30)
                scores.append(score[:, i * TILE : (i + 1) * TILE] + hide)
        tops = scores
        while len(tops) > 1:
            tops = [jnp.maximum(a, b) for a, b in zip(tops[0::2], tops[1::2])]
        return begin, gate, scores, jnp.max(tops[0], axis=1, keepdims=True)

    def mix(slot, begin, gate, scores, top):
        summed = None
        for j in range(0, most, CHUNK):
            weights = jnp.concatenate(
                [jnp.exp2((scores[j + i] - top) * rate).astype(jnp.bfloat16) for i in range(CHUNK)],
                axis=1,
            )
            block = jnp.concatenate([value_buf[begin + j + i] for i in range(CHUNK)], axis=0)
            term = jnp.dot(
                weights,
                jnp.concatenate([block, ones], axis=1),
                preferred_element_type=jnp.float32,
            )
            summed = term if summed is None else summed + term
        out_ref[slot] = (summed[:, 0:HD] / summed[:, HD:] * gate).astype(jnp.bfloat16)

    @pl.loop(0, chips // GROUP)
    def _(group):
        slots = [group * GROUP + i for i in range(GROUP)]
        states = [weigh(slot) for slot in slots]
        for slot, state in zip(slots, states):
            mix(slot, *state)


def return_kernel(chips, attended_ref, out_ref, land_buf, send_sem, recv_sem, local_sem):
    seq = lax.axis_index("seq")
    chip = lax.div(seq, 2)
    core = lax.rem(seq, 2)
    partner = {"seq": 2 * chip + 1 - core}
    ahead = others(chip, chips, 1)[::-1]
    behind = others(chip, chips, -1)[::-1]
    barrier = pltpu.get_barrier_semaphore()

    for other in behind:
        device = {"seq": 2 * other + core}
        pl.semaphore_signal(barrier, inc=1, device_id=device, device_id_type=MESH)

    own = pltpu.make_async_copy(attended_ref.at[chip], land_buf.at[chip], local_sem)
    own.start()

    pl.semaphore_wait(barrier, chips - 1)

    def out_copy(other):
        return remote(
            attended_ref.at[other],
            land_buf.at[chip],
            send_sem.at[other],
            recv_sem.at[chip],
            {"seq": 2 * other + core},
        )

    for other in behind:
        out_copy(other).start()

    own.wait()
    out_ref[:, columns(chip)] = land_buf[chip]

    for head in ahead:
        remote(
            land_buf.at[head], land_buf.at[head], send_sem.at[head], recv_sem.at[head], partner
        ).wait_recv()
        out_ref[:, columns(head)] = land_buf[head]

    for other in behind:
        out_copy(other).wait_send()


def per_device(query_rows, key_rows, value_rows, clip_tiles, conditioning, gate_weight):
    seq_count = lax.axis_size("seq")
    packs = lax.axis_size("dp")
    chips = seq_count // 2
    most = min(16, seq_count // 2)
    dma = pltpu.SemaphoreType.DMA
    vmem = pl.BlockSpec(memory_space=pltpu.VMEM)
    smem = pl.BlockSpec(memory_space=pltpu.SMEM)
    anywhere = pl.BlockSpec(memory_space=pl.ANY)
    part_shape = jax.ShapeDtypeStruct((chips, TILE, HD), jnp.bfloat16)
    whole_shape = jax.ShapeDtypeStruct((2 * chips, TILE, HD), jnp.bfloat16)

    gate_buf = pltpu.VMEM((packs, 8, HD), jnp.float32)
    query_all, key_all, value_all, gates = pl.pallas_call(
        functools.partial(gather_kernel, chips, packs),
        out_shape=[
            part_shape,
            whole_shape,
            whole_shape,
            jax.ShapeDtypeStruct((8, HD), jnp.float32),
        ],
        in_specs=[anywhere] * 3 + [vmem] * 2,
        out_specs=[anywhere] * 3 + [vmem],
        scratch_shapes=[gate_buf, gate_buf, pltpu.VMEM((2, 8, HD), jnp.float32)]
        + [dma((chips,))] * 10
        + [dma((3,)), dma((packs,)), dma((packs,)), dma, dma],
        compiler_params=pltpu.CompilerParams(collective_id=0, has_side_effects=True),
        name="gather_heads",
    )(query_rows, key_rows, value_rows, conditioning, gate_weight.T)

    attended = pl.pallas_call(
        functools.partial(attend_kernel, chips, most),
        out_shape=part_shape,
        in_specs=[smem, vmem, vmem, vmem, vmem],
        out_specs=vmem,
        compiler_params=pltpu.CompilerParams(vmem_limit_bytes=ATTEND_VMEM * 1024 * 1024),
        name="attend",
    )(clip_tiles, query_all, key_all, value_all, gates)

    return pl.pallas_call(
        functools.partial(return_kernel, chips),
        out_shape=jax.ShapeDtypeStruct(query_rows.shape, jnp.bfloat16),
        in_specs=[pl.BlockSpec(memory_space=pltpu.HBM)],
        out_specs=vmem,
        scratch_shapes=[
            pltpu.VMEM((chips, TILE, HD), jnp.bfloat16),
            dma((chips,)),
            dma((chips,)),
            dma,
        ],
        compiler_params=pltpu.CompilerParams(
            collective_id=1, has_side_effects=True, vmem_limit_bytes=16 * 1024 * 1024
        ),
        name="return_tiles",
    )(attended)


def solution(mesh):
    return jax.shard_map(
        per_device,
        mesh=mesh,
        in_specs=(
            P(("dp", "seq"), None),
            P(("dp", "seq"), None),
            P(("dp", "seq"), None),
            P("dp", None),
            P(None, "dp"),
            P("dp", "seq"),
        ),
        out_specs=P(("dp", "seq"), None),
        check_vma=False,
    )
```

```python
import functools
import math

import jax
import jax.numpy as jnp
from jax import lax
from jax.experimental import pallas as pl
from jax.experimental.pallas import tpu as pltpu
from jax.sharding import PartitionSpec as P

HD = 128
TILE = 128
CLIPS = 4
CHUNK = 2
GROUP = 8
ATTEND_VMEM = 60
LOG2E = 1.4426950408889634
MESH = pl.DeviceIdType.MESH


def remote(src, dst, send_sem, recv_sem, device):
    return pltpu.make_async_remote_copy(
        src_ref=src,
        dst_ref=dst,
        send_sem=send_sem,
        recv_sem=recv_sem,
        device_id=device,
        device_id_type=MESH,
    )


def columns(head):
    return pl.ds(pl.multiple_of(head * HD, HD), HD)


def others(chip, chips, sign):
    side = chips // 2
    x, y = lax.div(chip, side), lax.rem(chip, side)
    found = []
    for turn in range(side):
        far = (turn + 1) // 2 if turn % 2 else (side - turn // 2) % side
        row = lax.rem(y + (far if sign > 0 else side - far), side)
        for cross in range(2):
            if turn or cross:
                found.append(lax.rem(x + cross, 2) * side + row)
    return found


def gather_kernel(
    chips,
    packs,
    query_ref,
    key_ref,
    value_ref,
    cond_ref,
    weight_ref,
    query_out,
    key_out,
    value_out,
    gate_out,
    gate_send,
    gate_recv,
    gate_half,
    query_send_sem,
    key_send_sem,
    value_send_sem,
    query_recv_sem,
    key_recv_sem,
    value_recv_sem,
    key_relay_send_sem,
    value_relay_send_sem,
    key_relay_recv_sem,
    value_relay_recv_sem,
    local_sem,
    gate_send_sem,
    gate_recv_sem,
    half_send_sem,
    half_recv_sem,
):
    pack = lax.axis_index("dp")
    seq = lax.axis_index("seq")
    chip = lax.div(seq, 2)
    core = lax.rem(seq, 2)
    own_tile = seq
    partner = {"seq": 2 * chip + 1 - core}
    ahead = others(chip, chips, 1)
    behind = others(chip, chips, -1)
    packs_ahead = [lax.rem(pack + k, packs) for k in range(1, packs)]

    barrier = pltpu.get_barrier_semaphore()

    for head in ahead:
        other = {"seq": 2 * head + core}
        pl.semaphore_signal(barrier, inc=1, device_id=other, device_id_type=MESH)

    pl.semaphore_signal(barrier, inc=1, device_id=partner, device_id_type=MESH)
    for other in packs_ahead:
        pl.semaphore_signal(barrier, inc=1, device_id={"dp": other}, device_id_type=MESH)

    own_key = pltpu.make_async_copy(
        key_ref.at[:, columns(chip)], key_out.at[own_tile], local_sem.at[0]
    )
    own_value = pltpu.make_async_copy(
        value_ref.at[:, columns(chip)], value_out.at[own_tile], local_sem.at[1]
    )
    own_query = pltpu.make_async_copy(
        query_ref.at[:, columns(chip)], query_out.at[chip], local_sem.at[2]
    )
    own_key.start()
    own_value.start()
    own_query.start()

    cond = cond_ref[...].astype(jnp.float32)
    act = (cond / (1.0 + jnp.exp(-cond))).astype(jnp.bfloat16)
    part = lax.dot_general(
        act, weight_ref[...], (((1,), (1,)), ((), ())), preferred_element_type=jnp.float32
    )
    gate_send[...] = jnp.zeros_like(gate_send)
    for p in range(packs):
        gate_send[p, 0:CLIPS, 0 : HD // 2] = part[p * CLIPS : (p + 1) * CLIPS, :]
    gate_recv[pack] = gate_send[pack]

    pl.semaphore_wait(barrier, chips + packs - 1)

    def shift(source, target, slot, send_sem, recv_sem, head):
        return remote(
            source.at[:, columns(head)],
            target.at[slot],
            send_sem.at[head],
            recv_sem.at[chip],
            {"seq": 2 * head + core},
        )

    def key_copy(head):
        return shift(key_ref, key_out, own_tile, key_send_sem, key_recv_sem, head)

    def value_copy(head):
        return shift(value_ref, value_out, own_tile, value_send_sem, value_recv_sem, head)

    def query_copy(head):
        return shift(query_ref, query_out, chip, query_send_sem, query_recv_sem, head)

    def relay(target, tile, send_sem, recv_sem):
        return remote(target.at[tile], target.at[tile], send_sem, recv_sem, partner)

    def key_relay(source):
        return relay(
            key_out,
            2 * source + core,
            key_relay_send_sem.at[source],
            key_relay_recv_sem.at[source],
        )

    def value_relay(source):
        return relay(
            value_out,
            2 * source + core,
            value_relay_send_sem.at[source],
            value_relay_recv_sem.at[source],
        )

    def arrived(buffer, slot, sem):
        remote(buffer.at[slot], buffer.at[slot], sem, sem, partner).wait_recv()

    def gate_copy(other):
        return remote(
            gate_send.at[other],
            gate_recv.at[pack],
            gate_send_sem.at[other],
            gate_recv_sem.at[pack],
            {"dp": other},
        )

    for head in ahead:
        key_copy(head).start()
    own_key.wait()
    key_relay(chip).start()
    for head in ahead:
        value_copy(head).start()
    own_value.wait()
    value_relay(chip).start()
    for head in ahead:
        query_copy(head).start()
    for other in packs_ahead:
        gate_copy(other).start()

    for source in behind:
        arrived(key_out, 2 * source + core, key_recv_sem.at[source])
        key_relay(source).start()

    for source in packs_ahead:
        arrived(gate_recv, source, gate_recv_sem.at[source])
    gate_half[core] = jnp.sum(gate_recv[...], axis=0)
    half_copy = remote(
        gate_half.at[core], gate_half.at[core], half_send_sem, half_recv_sem, partner
    )
    half_copy.start()

    for source in behind:
        arrived(value_out, 2 * source + core, value_recv_sem.at[source])
        value_relay(source).start()

    arrived(gate_half, 1 - core, half_recv_sem)
    gate_out[...] = jnp.concatenate(
        [gate_half[0, :, 0 : HD // 2], gate_half[1, :, 0 : HD // 2]], axis=1
    )
    half_copy.wait_send()
    for other in packs_ahead:
        gate_copy(other).wait_send()

    own_query.wait()
    for head in ahead:
        key_copy(head).wait_send()
        value_copy(head).wait_send()
        query_copy(head).wait_send()
    for source in behind:
        arrived(query_out, source, query_recv_sem.at[source])

    for source in behind + [chip]:
        tile = 2 * source + 1 - core
        arrived(key_out, tile, key_relay_recv_sem.at[source])
        arrived(value_out, tile, value_relay_recv_sem.at[source])
        key_relay(source).wait_send()
        value_relay(source).wait_send()


def attend_kernel(
    chips,
    most,
    clip_ref,
    query_buf,
    key_buf,
    value_buf,
    gate_ref,
    out_ref,
):
    seq = lax.axis_index("seq")
    core = seq % 2
    tiles = 2 * chips
    def count(j, found):
        clip = clip_ref[0, j]
        return tuple(
            found[c] + jnp.where(clip < c + 1, 1, 0).astype(jnp.int32) for c in range(CLIPS - 1)
        )

    begins = lax.fori_loop(0, tiles, count, (jnp.int32(0),) * (CLIPS - 1))
    rate = LOG2E / math.sqrt(HD)
    ones = jnp.ones((CHUNK * TILE, HD), jnp.bfloat16)

    gates = gate_ref[...]

    def weigh(source):
        clip = clip_ref[0, 2 * source + core]
        begin = jnp.int32(0)
        gate = gates[0:1, :]
        for c in range(1, CLIPS):
            begin = jnp.where(clip == c, begins[c - 1], begin)
            gate = jnp.where(clip == c, gates[c : c + 1, :], gate)
        begin = jnp.minimum(begin, tiles - most)
        query = query_buf[source]
        scores = []
        for j in range(0, most, CHUNK):
            block = jnp.concatenate([key_buf[begin + j + i] for i in range(CHUNK)], axis=0)
            score = lax.dot_general(
                query, block, (((1,), (1,)), ((), ())), preferred_element_type=jnp.float32
            )
            for i in range(CHUNK):
                hide = jnp.where(clip_ref[0, begin + j + i] == clip, 0.0, -1e30)
                scores.append(score[:, i * TILE : (i + 1) * TILE] + hide)
        tops = scores
        while len(tops) > 1:
            tops = [jnp.maximum(a, b) for a, b in zip(tops[0::2], tops[1::2])]
        return begin, gate, scores, jnp.max(tops[0], axis=1, keepdims=True)

    def mix(slot, begin, gate, scores, top):
        summed = None
        for j in range(0, most, CHUNK):
            weights = jnp.concatenate(
                [jnp.exp2((scores[j + i] - top) * rate).astype(jnp.bfloat16) for i in range(CHUNK)],
                axis=1,
            )
            block = jnp.concatenate([value_buf[begin + j + i] for i in range(CHUNK)], axis=0)
            term = jnp.dot(
                weights,
                jnp.concatenate([block, ones], axis=1),
                preferred_element_type=jnp.float32,
            )
            summed = term if summed is None else summed + term
        out_ref[slot] = (summed[:, 0:HD] / summed[:, HD:] * gate).astype(jnp.bfloat16)

    @pl.loop(0, chips // GROUP)
    def _(group):
        slots = [group * GROUP + i for i in range(GROUP)]
        states = [weigh(slot) for slot in slots]
        for slot, state in zip(slots, states):
            mix(slot, *state)


def return_kernel(chips, attended_ref, out_ref, land_buf, send_sem, recv_sem, local_sem):
    seq = lax.axis_index("seq")
    chip = lax.div(seq, 2)
    core = lax.rem(seq, 2)
    partner = {"seq": 2 * chip + 1 - core}
    ahead = others(chip, chips, 1)[::-1]
    behind = others(chip, chips, -1)[::-1]
    barrier = pltpu.get_barrier_semaphore()

    for other in behind:
        device = {"seq": 2 * other + core}
        pl.semaphore_signal(barrier, inc=1, device_id=device, device_id_type=MESH)

    own = pltpu.make_async_copy(attended_ref.at[chip], land_buf.at[chip], local_sem)
    own.start()

    pl.semaphore_wait(barrier, chips - 1)

    def out_copy(other):
        return remote(
            attended_ref.at[other],
            land_buf.at[chip],
            send_sem.at[other],
            recv_sem.at[chip],
            {"seq": 2 * other + core},
        )

    for other in behind:
        out_copy(other).start()

    own.wait()
    out_ref[:, columns(chip)] = land_buf[chip]

    for head in ahead:
        remote(
            land_buf.at[head], land_buf.at[head], send_sem.at[head], recv_sem.at[head], partner
        ).wait_recv()
        out_ref[:, columns(head)] = land_buf[head]

    for other in behind:
        out_copy(other).wait_send()


def per_device(query_rows, key_rows, value_rows, clip_tiles, conditioning, gate_weight):
    seq_count = lax.axis_size("seq")
    packs = lax.axis_size("dp")
    chips = seq_count // 2
    most = min(16, seq_count // 2)
    dma = pltpu.SemaphoreType.DMA
    vmem = pl.BlockSpec(memory_space=pltpu.VMEM)
    smem = pl.BlockSpec(memory_space=pltpu.SMEM)
    anywhere = pl.BlockSpec(memory_space=pl.ANY)
    part_shape = jax.ShapeDtypeStruct((chips, TILE, HD), jnp.bfloat16)
    whole_shape = jax.ShapeDtypeStruct((2 * chips, TILE, HD), jnp.bfloat16)

    gate_buf = pltpu.VMEM((packs, 8, HD), jnp.float32)
    query_all, key_all, value_all, gates = pl.pallas_call(
        functools.partial(gather_kernel, chips, packs),
        out_shape=[
            part_shape,
            whole_shape,
            whole_shape,
            jax.ShapeDtypeStruct((8, HD), jnp.float32),
        ],
        in_specs=[anywhere] * 3 + [vmem] * 2,
        out_specs=[anywhere] * 3 + [vmem],
        scratch_shapes=[gate_buf, gate_buf, pltpu.VMEM((2, 8, HD), jnp.float32)]
        + [dma((chips,))] * 10
        + [dma((3,)), dma((packs,)), dma((packs,)), dma, dma],
        compiler_params=pltpu.CompilerParams(collective_id=0, has_side_effects=True),
        name="gather_heads",
    )(query_rows, key_rows, value_rows, conditioning, gate_weight.T)

    attended = pl.pallas_call(
        functools.partial(attend_kernel, chips, most),
        out_shape=part_shape,
        in_specs=[smem, vmem, vmem, vmem, vmem],
        out_specs=vmem,
        compiler_params=pltpu.CompilerParams(vmem_limit_bytes=ATTEND_VMEM * 1024 * 1024),
        name="attend",
    )(clip_tiles, query_all, key_all, value_all, gates)

    return pl.pallas_call(
        functools.partial(return_kernel, chips),
        out_shape=jax.ShapeDtypeStruct(query_rows.shape, jnp.bfloat16),
        in_specs=[pl.BlockSpec(memory_space=pltpu.HBM)],
        out_specs=vmem,
        scratch_shapes=[
            pltpu.VMEM((chips, TILE, HD), jnp.bfloat16),
            dma((chips,)),
            dma((chips,)),
            dma,
        ],
        compiler_params=pltpu.CompilerParams(
            collective_id=1, has_side_effects=True, vmem_limit_bytes=16 * 1024 * 1024
        ),
        name="return_tiles",
    )(attended)


def solution(mesh):
    return jax.shard_map(
        per_device,
        mesh=mesh,
        in_specs=(
            P(("dp", "seq"), None),
            P(("dp", "seq"), None),
            P(("dp", "seq"), None),
            P("dp", None),
            P(None, "dp"),
            P("dp", "seq"),
        ),
        out_specs=P(("dp", "seq"), None),
        check_vma=False,
    )
```
